32 devices in a mesh: replica: 8 (over y, x, core), fsdp: 4 (over z).
Axes of the slice: x: 2, y: 2, z: 4, core: 2. Of those that a mesh axis runs over, the one named last changes fastest.
Arguments:
- tokens: bfloat16 [12288, 2048], P(('replica', 'fsdp')), may hold values from -24 to 24
- cotangent: bfloat16 [12288, 2048], P(('replica', 'fsdp')), may hold values from -6 to 6
- w_query: bfloat16 [8, 2048, 2048], P('replica', 'fsdp'), may hold values from -0.125 to 0.125
- replica_key_weight: bfloat16 [8, 2048, 512], P('replica', 'fsdp'), may hold values from -0.125 to 0.125
- replica_value_weight: bfloat16 [8, 2048, 512], P('replica', 'fsdp'), may hold values from -0.125 to 0.125
- w_output: bfloat16 [8, 2048, 2048], P('replica', None, 'fsdp'), may hold values from -0.125 to 0.125
- snapshot: bfloat16 [8, 2048, 2048], P('replica', None, 'fsdp'), may hold values from -0.1875 to 0.1875
- global_output: float32 [2048, 2048], P('replica', 'fsdp'), may hold values from -0.125 to 0.125
- momentum: float32 [2048, 2048], P('replica', 'fsdp'), may hold values from -0.18 to 0.18
Outputs:
- block_out: bfloat16 [12288, 2048], P(('replica', 'fsdp'))
- grad_query: bfloat16 [8, 2048, 2048], P('replica', 'fsdp')
- grad_key: bfloat16 [8, 2048, 512], P('replica', 'fsdp')
- grad_value: bfloat16 [8, 2048, 512], P('replica', 'fsdp')
- grad_output: bfloat16 [8, 2048, 2048], P('replica', None, 'fsdp')
- merged_output: bfloat16 [8, 2048, 2048], P('replica', None, 'fsdp')
- global_new: float32 [2048, 2048], P('replica', 'fsdp')
- momentum_new: float32 [2048, 2048], P('replica', 'fsdp')
The draws below stay inside these ranges and needn't reach their ends.
All inputs are finite; a program needn't handle non-finite values.
Results may differ from the reference program's by a relative error of at most 0.015.
The reference program's roundings to bfloat16 on the way count: a program that leaves them out, or rounds other values in their place, can miss the bound.
Values may be sent and summed in bfloat16 or wider, within the bound.
A program may use at most 192 MiB of HBM per device.

```python
import jax
import jax.numpy as jnp
from jax import lax

MODEL_WIDTH = 2048
HEAD_SIZE = 128
QUERY_HEADS = 16
KEYVALUE_HEADS = 4
DEVICE_TOKENS = 384
TOKENS = 12288
N_REPLICA = 8
N_FSDP = 4


def draw_tokens(key, part):
    key = jax.random.fold_in(key, 11)
    first = jax.random.fold_in(key, 0)
    drawn = jax.random.normal(first, (TOKENS, MODEL_WIDTH), jnp.float32)
    return jnp.clip(drawn, -24.0, 24.0).astype(jnp.bfloat16)


def spiked(result, stream_key, source, target, shards_of, factor):
    def block_of(dim):
        return (jnp.arange(result.shape[dim]) // (result.shape[dim] // shards_of)).reshape((-1,) + (1,) * (result.ndim - 1 - dim))

    one_side = jax.random.permutation(stream_key, shards_of)[block_of(target)]
    far = (block_of(target) + shards_of // 2) % shards_of
    return jnp.where((block_of(source) == one_side) | (block_of(source) == far), factor * result, result)


def block_scale(key, dims, cuts, smallest, largest):
    factor_of = 1.0
    for dim, blocks in cuts:
        heights = jax.random.uniform(jax.random.fold_in(jax.random.fold_in(key, 6), dim), (blocks,), jnp.float32, smallest / len(cuts), largest / len(cuts))
        factor_of = factor_of * jnp.repeat(jnp.exp(heights), dims[dim] // blocks).reshape((-1,) + (1,) * (len(dims) - 1 - dim))
    return factor_of


def normal_values(key, extent, width, reach, pieces=(), held_as=jnp.bfloat16):
    array = width * jax.random.normal(key, extent, jnp.float32)
    if pieces:
        array = array * block_scale(key, extent, pieces, -0.22, 0.18)
    return jnp.clip(array, -reach, reach).astype(held_as)


def bell_draw_with(rng, shape, width, bound, cuts, heavy, kind=jnp.bfloat16):
    values = width * jax.random.normal(rng, shape, jnp.float32)
    if cuts:
        values = values * block_scale(rng, shape, cuts, -0.22, 0.18)
    return jnp.clip(spiked(values, jax.random.fold_in(rng, 3), *heavy), -bound, bound).astype(kind)


def setup_inputs(seed: int = 0) -> dict:
    keys = jax.random.split(jax.random.key(seed), 10)
    return {
        "tokens": draw_tokens(jax.random.fold_in(keys[9], 71), 0),
        "cotangent": normal_values(keys[1], (TOKENS, MODEL_WIDTH), 1.0, 6.0, ((0, 32),)),
        "w_query": normal_values(keys[2], (N_REPLICA, MODEL_WIDTH, QUERY_HEADS * HEAD_SIZE), MODEL_WIDTH ** -0.5, 0.125, ((0, 8), (1, 4))),
        "replica_key_weight": normal_values(keys[3], (N_REPLICA, MODEL_WIDTH, KEYVALUE_HEADS * HEAD_SIZE), MODEL_WIDTH ** -0.5, 0.125, ((0, 8), (1, 4))),
        "replica_value_weight": normal_values(keys[4], (N_REPLICA, MODEL_WIDTH, KEYVALUE_HEADS * HEAD_SIZE), MODEL_WIDTH ** -0.5, 0.125, ((0, 8), (1, 4))),
        "w_output": normal_values(keys[5], (N_REPLICA, QUERY_HEADS * HEAD_SIZE, MODEL_WIDTH), (QUERY_HEADS * HEAD_SIZE) ** -0.5, 0.125, ((0, 8), (2, 4))),
        "snapshot": bell_draw_with(keys[6], (N_REPLICA, QUERY_HEADS * HEAD_SIZE, MODEL_WIDTH), (QUERY_HEADS * HEAD_SIZE) ** -0.5, 0.1875, ((0, 8), (2, 4)), (0, 1, 8, 2.0)),
        "global_output": normal_values(keys[7], (QUERY_HEADS * HEAD_SIZE, MODEL_WIDTH), (QUERY_HEADS * HEAD_SIZE) ** -0.5, 0.125, ((0, 8), (1, 4)), jnp.float32),
        "momentum": normal_values(keys[8], (QUERY_HEADS * HEAD_SIZE, MODEL_WIDTH), 0.03, 0.18, ((0, 8), (1, 4)), jnp.float32),
    }


theta_base = 500000.0
momentum_decay = 0.9
outer_rate = 0.7
mixing = 0.5


def apply_rotation(value_rows, sign):
    sequence_length = value_rows.shape[0]
    half = value_rows.shape[2] // 2
    position = jnp.arange(sequence_length).astype(jnp.float32)
    freq = jnp.exp(-jnp.log(theta_base) * jnp.arange(half).astype(jnp.float32) * 2.0 / value_rows.shape[2])
    angle = position[:, None] * freq[None, :]
    cosine = jnp.cos(angle)[:, None, :]
    sine = sign * jnp.sin(angle)[:, None, :]
    first = value_rows[..., :half]
    second = value_rows[..., half:]
    return jnp.concatenate([first * cosine - second * sine, first * sine + second * cosine], axis=-1)


def attend_forward(query_unrotated, key_unrotated, value_unprojected):
    sequence_length = query_unrotated.shape[0]
    head_group = QUERY_HEADS // KEYVALUE_HEADS
    scale = HEAD_SIZE ** -0.5
    query_rows = apply_rotation(query_unrotated.reshape(sequence_length, QUERY_HEADS, HEAD_SIZE), 1.0).astype(jnp.bfloat16).reshape(sequence_length, KEYVALUE_HEADS, head_group, HEAD_SIZE)
    key_rows = apply_rotation(key_unrotated.reshape(sequence_length, KEYVALUE_HEADS, HEAD_SIZE), 1.0).astype(jnp.bfloat16)
    value_rows = value_unprojected.astype(jnp.bfloat16).reshape(sequence_length, KEYVALUE_HEADS, HEAD_SIZE)
    scores = jnp.einsum("qkgd,skd->kgqs", query_rows.astype(jnp.float32), key_rows.astype(jnp.float32)) * scale
    causal = jnp.arange(sequence_length)[:, None] >= jnp.arange(sequence_length)[None, :]
    scores = jnp.where(causal, scores, -1e30)
    top = jnp.max(scores, axis=-1, keepdims=True)
    expo = jnp.exp(scores - top)
    probs = expo / jnp.sum(expo, axis=-1, keepdims=True)
    probs_b = probs.astype(jnp.bfloat16)
    attn = jnp.einsum("kgqs,skd->qkgd", probs_b.astype(jnp.float32), value_rows.astype(jnp.float32))
    attn = attn.astype(jnp.bfloat16).reshape(sequence_length, QUERY_HEADS * HEAD_SIZE)
    return attn, (query_rows, key_rows, value_rows, probs, probs_b)


def attend_backward(saved, attention_gradient):
    query_rows, key_rows, value_rows, probs, probs_b = saved
    sequence_length = query_rows.shape[0]
    head_group = QUERY_HEADS // KEYVALUE_HEADS
    scale = HEAD_SIZE ** -0.5
    output_gradient = attention_gradient.reshape(sequence_length, KEYVALUE_HEADS, head_group, HEAD_SIZE).astype(jnp.float32)
    value_gradient = jnp.einsum("kgqs,qkgd->skd", probs_b.astype(jnp.float32), output_gradient)
    d_probs = jnp.einsum("qkgd,skd->kgqs", output_gradient, value_rows.astype(jnp.float32))
    d_scores = (probs * (d_probs - jnp.sum(d_probs * probs, axis=-1, keepdims=True))).astype(jnp.bfloat16)
    query_gradient = jnp.einsum("kgqs,skd->qkgd", d_scores.astype(jnp.float32), key_rows.astype(jnp.float32)) * scale
    key_gradient = jnp.einsum("kgqs,qkgd->skd", d_scores.astype(jnp.float32), query_rows.astype(jnp.float32)) * scale
    query_gradient = apply_rotation(query_gradient.reshape(sequence_length, QUERY_HEADS, HEAD_SIZE), -1.0).reshape(sequence_length, QUERY_HEADS * HEAD_SIZE)
    key_gradient = apply_rotation(key_gradient, -1.0).reshape(sequence_length, KEYVALUE_HEADS * HEAD_SIZE)
    projection_gradient = jnp.concatenate([query_gradient, key_gradient, value_gradient.reshape(sequence_length, KEYVALUE_HEADS * HEAD_SIZE)], axis=1)
    return projection_gradient.astype(jnp.bfloat16)


def replica_step(packed):
    inputs, upstream, w_q, key_matrix, value_matrix, w_o = packed
    flattened = inputs.reshape(N_FSDP * DEVICE_TOKENS, MODEL_WIDTH)
    query_unrotated = jnp.dot(flattened, w_q, preferred_element_type=jnp.float32).reshape(N_FSDP, DEVICE_TOKENS, QUERY_HEADS * HEAD_SIZE)
    key_unrotated = jnp.dot(flattened, key_matrix, preferred_element_type=jnp.float32).reshape(N_FSDP, DEVICE_TOKENS, KEYVALUE_HEADS * HEAD_SIZE)
    value_unprojected = jnp.dot(flattened, value_matrix, preferred_element_type=jnp.float32).reshape(N_FSDP, DEVICE_TOKENS, KEYVALUE_HEADS * HEAD_SIZE)
    attn, saved = jax.vmap(attend_forward)(query_unrotated, key_unrotated, value_unprojected)
    attn_flat = attn.reshape(N_FSDP * DEVICE_TOKENS, QUERY_HEADS * HEAD_SIZE)
    output_rows = (flattened.astype(jnp.float32) + jnp.dot(attn_flat, w_o, preferred_element_type=jnp.float32)).astype(jnp.bfloat16)
    up_flat = upstream.reshape(N_FSDP * DEVICE_TOKENS, MODEL_WIDTH)
    attention_gradient = jnp.dot(up_flat, w_o.T, preferred_element_type=jnp.float32).astype(jnp.bfloat16)
    projection_gradient = jax.vmap(attend_backward)(saved, attention_gradient.reshape(N_FSDP, DEVICE_TOKENS, QUERY_HEADS * HEAD_SIZE))
    terms_in = jnp.einsum("fsd,fse->fde", inputs.astype(jnp.float32), projection_gradient.astype(jnp.float32)).astype(jnp.bfloat16)
    gradient_incoming = jnp.sum(terms_in.astype(jnp.float32), axis=0).astype(jnp.bfloat16)
    terms_out = jnp.einsum("fsh,fsd->fhd", attn.astype(jnp.float32), upstream.astype(jnp.float32)).astype(jnp.bfloat16)
    gradient_outgoing = jnp.sum(terms_out.astype(jnp.float32), axis=0).astype(jnp.bfloat16)
    return output_rows, gradient_incoming[:, :QUERY_HEADS * HEAD_SIZE], gradient_incoming[:, QUERY_HEADS * HEAD_SIZE:(QUERY_HEADS + KEYVALUE_HEADS) * HEAD_SIZE], gradient_incoming[:, (QUERY_HEADS + KEYVALUE_HEADS) * HEAD_SIZE:], gradient_outgoing


def reference(tokens, cotangent, w_query, replica_key_weight, replica_value_weight, w_output, snapshot, global_output, momentum):
    inputs = tokens.reshape(N_REPLICA, N_FSDP, DEVICE_TOKENS, MODEL_WIDTH)
    upstream = cotangent.reshape(N_REPLICA, N_FSDP, DEVICE_TOKENS, MODEL_WIDTH)
    output_rows, grad_query, grad_key, grad_value, grad_output = lax.map(
        replica_step, (inputs, upstream, w_query, replica_key_weight, replica_value_weight, w_output))
    block_out = output_rows.reshape(N_REPLICA * N_FSDP * DEVICE_TOKENS, MODEL_WIDTH)
    mean_snapshot = jnp.sum(snapshot.astype(jnp.float32), axis=0) / N_REPLICA
    delta = global_output - mean_snapshot
    momentum_new = momentum_decay * momentum + delta
    global_new = global_output - outer_rate * (delta + momentum_decay * momentum_new)
    merged_output = (mixing * w_output.astype(jnp.float32) + (1.0 - mixing) * global_new[None]).astype(jnp.bfloat16)
    return block_out, grad_query, grad_key, grad_value, grad_output, merged_output, global_new, momentum_new
```

```python
import jax
import jax.numpy as jnp
from jax import lax
from jax.sharding import PartitionSpec as P

HEAD_SIZE = 128
QUERY_HEADS = 16
KEYVALUE_HEADS = 4


theta_base = 500000.0
momentum_decay = 0.9
outer_rate = 0.7
mixing = 0.5


def apply_rotation(value_rows, sign):
    sequence_length = value_rows.shape[0]
    half = value_rows.shape[2] // 2
    position = jnp.arange(sequence_length).astype(jnp.float32)
    freq = jnp.exp(
        -jnp.log(theta_base) * jnp.arange(half).astype(jnp.float32) * 2.0 / value_rows.shape[2]
    )
    angle = position[:, None] * freq[None, :]
    cosine = jnp.cos(angle)[:, None, :]
    sine = sign * jnp.sin(angle)[:, None, :]
    first = value_rows[..., :half]
    second = value_rows[..., half:]
    return jnp.concatenate(
        [first * cosine - second * sine, first * sine + second * cosine], axis=-1
    )


def rotate(value_rows, sign):
    return jax.vmap(lambda rows: apply_rotation(rows, sign))(value_rows)


def gather(block):
    return lax.all_gather(block, "fsdp", axis=0, tiled=True)


def attend(query_raw, key_raw, value_raw):
    scale = HEAD_SIZE ** (-0.5)
    query_rows = rotate(query_raw, 1.0).astype(jnp.bfloat16)
    key_rows = rotate(key_raw[:, :, None, :], 1.0)[:, :, 0].astype(jnp.bfloat16)
    value_rows = value_raw.astype(jnp.bfloat16)
    length = query_raw.shape[1]
    scores = (
        jnp.einsum("sqgd,skd->sgqk", query_rows, key_rows, preferred_element_type=jnp.float32)
        * scale
    )
    causal = jnp.arange(length)[:, None] >= jnp.arange(length)[None, :]
    scores = jnp.where(causal, scores, -1e30)
    top = jnp.max(scores, axis=-1, keepdims=True)
    expo = jnp.exp(scores - top)
    probs = expo / jnp.sum(expo, axis=-1, keepdims=True)
    probs_b = probs.astype(jnp.bfloat16)
    attn = jnp.einsum("sgqk,skd->sqgd", probs_b, value_rows, preferred_element_type=jnp.float32)
    return attn.astype(jnp.bfloat16), (query_rows, key_rows, value_rows, probs, probs_b)


def attend_gradient(saved, d_attn):
    query_rows, key_rows, value_rows, probs, probs_b = saved
    scale = HEAD_SIZE ** (-0.5)
    d_values = jnp.einsum("sgqk,sqgd->skd", probs_b, d_attn, preferred_element_type=jnp.float32)
    d_probs = jnp.einsum("sqgd,skd->sgqk", d_attn, value_rows, preferred_element_type=jnp.float32)
    d_scores = (probs * (d_probs - jnp.sum(d_probs * probs, axis=-1, keepdims=True))).astype(
        jnp.bfloat16
    )
    d_queries = (
        jnp.einsum("sgqk,skd->sqgd", d_scores, key_rows, preferred_element_type=jnp.float32) * scale
    )
    d_keys = (
        jnp.einsum("sgqk,sqgd->skd", d_scores, query_rows, preferred_element_type=jnp.float32)
        * scale
    )
    d_queries = rotate(d_queries, -1.0)
    d_keys = rotate(d_keys[:, :, None, :], -1.0)[:, :, 0]
    rows = d_attn.shape[0] * d_attn.shape[1]
    return jnp.concatenate(
        [part.astype(jnp.bfloat16).reshape(rows, -1) for part in (d_queries, d_keys, d_values)],
        axis=1,
    )


def exchange(pick, place, out):
    n = lax.axis_size("fsdp")
    me = lax.axis_index("fsdp")
    out = place(out, pick(me), me)
    for shift in range(1, n):
        pairs = [(f, (f + shift) % n) for f in range(n)]
        piece = lax.ppermute(pick(lax.rem(me + shift, n)), "fsdp", pairs)
        out = place(out, piece, lax.rem(me + n - shift, n))
    return out


def outer_sync(snapshot, global_output, momentum, w_output):
    total = lax.psum_scatter(
        snapshot[0].astype(jnp.float32), "replica", scatter_dimension=0, tiled=True
    )
    mean_snapshot = total / lax.axis_size("replica")
    delta = global_output - mean_snapshot
    momentum_new = momentum_decay * momentum + delta
    global_new = global_output - outer_rate * (delta + momentum_decay * momentum_new)
    gathered = lax.all_gather(global_new, "replica", axis=0, tiled=True)
    merged = (mixing * w_output[0].astype(jnp.float32) + (1.0 - mixing) * gathered).astype(
        jnp.bfloat16
    )
    return (merged[None], global_new, momentum_new)


def per_device(
    tokens,
    cotangent,
    w_query,
    replica_key_weight,
    replica_value_weight,
    w_output,
    snapshot,
    global_output,
    momentum,
):
    n = lax.axis_size("fsdp")
    me = lax.axis_index("fsdp")
    length, width = tokens.shape
    depth = w_query.shape[1]
    own_query = w_query.shape[2] // n
    own_key = replica_key_weight.shape[2] // n
    own_cols = own_query + 2 * own_key
    group = own_query // HEAD_SIZE
    model_cols = w_output.shape[2]
    total_rows = n * length

    all_tokens = gather(tokens)
    all_cotangent = gather(cotangent)

    def pick_weight(d):
        return jnp.concatenate(
            [
                lax.dynamic_slice_in_dim(w_query[0], d * own_query, own_query, 1),
                lax.dynamic_slice_in_dim(replica_key_weight[0], d * own_key, own_key, 1),
                lax.dynamic_slice_in_dim(replica_value_weight[0], d * own_key, own_key, 1),
            ],
            axis=1,
        )

    def place_rows(out, piece, f):
        return lax.dynamic_update_slice_in_dim(out, piece, f * piece.shape[0], 0)

    def place_cols(out, piece, f):
        return lax.dynamic_update_slice_in_dim(out, piece, f * piece.shape[1], 1)

    w_in = exchange(pick_weight, place_rows, jnp.zeros((n * depth, own_cols), jnp.bfloat16))
    w_out_rows = exchange(
        lambda d: lax.dynamic_slice_in_dim(w_output[0], d * own_query, own_query, 0),
        place_cols,
        jnp.zeros((own_query, n * model_cols), jnp.bfloat16),
    )

    raw = jnp.dot(all_tokens, w_in, preferred_element_type=jnp.float32)
    query_raw = raw[:, :own_query].reshape(n, length, group, HEAD_SIZE)
    key_raw = raw[:, own_query : own_query + own_key].reshape(n, length, HEAD_SIZE)
    value_raw = raw[:, own_query + own_key :].reshape(n, length, HEAD_SIZE)
    attn, saved = attend(query_raw, key_raw, value_raw)

    own_attn = attn.reshape(total_rows, own_query)
    all_attn = lax.all_gather(own_attn, "fsdp", axis=1, tiled=True)

    d_attn = (
        lax.dot_general(
            all_cotangent,
            w_out_rows,
            (((1,), (1,)), ((), ())),
            preferred_element_type=jnp.float32,
        )
        .astype(jnp.bfloat16)
        .reshape(n, length, group, HEAD_SIZE)
    )
    d_in = attend_gradient(saved, d_attn)
    grad_in = lax.dot_general(
        all_tokens, d_in, (((0,), (0,)), ((), ())), preferred_element_type=jnp.float32
    ).astype(jnp.bfloat16)

    def place_grads(outs, piece, f):
        grad_query, grad_key, grad_value = outs
        return (
            place_cols(grad_query, piece[:, :own_query], f),
            place_cols(grad_key, piece[:, own_query : own_query + own_key], f),
            place_cols(grad_value, piece[:, own_query + own_key :], f),
        )

    grad_query, grad_key, grad_value = exchange(
        lambda d: lax.dynamic_slice_in_dim(grad_in, d * depth, depth, 0),
        place_grads,
        tuple(
            jnp.zeros(w.shape[1:], jnp.bfloat16)
            for w in (w_query, replica_key_weight, replica_value_weight)
        ),
    )

    own_token_cols = lax.dynamic_slice_in_dim(all_tokens, me * model_cols, model_cols, 1)
    out_cols = (
        own_token_cols.astype(jnp.float32)
        + jnp.dot(all_attn, w_output[0], preferred_element_type=jnp.float32)
    ).astype(jnp.bfloat16)
    block_out = exchange(
        lambda d: lax.dynamic_slice_in_dim(out_cols, d * length, length, 0),
        place_cols,
        jnp.zeros((length, width), jnp.bfloat16),
    )
    own_cotangent_cols = lax.dynamic_slice_in_dim(all_cotangent, me * model_cols, model_cols, 1)
    grad_output = lax.dot_general(
        all_attn, own_cotangent_cols, (((0,), (0,)), ((), ())), preferred_element_type=jnp.float32
    ).astype(jnp.bfloat16)

    merged_output, global_new, momentum_new = outer_sync(
        snapshot, global_output, momentum, w_output
    )
    return (
        block_out,
        grad_query[None],
        grad_key[None],
        grad_value[None],
        grad_output[None],
        merged_output,
        global_new,
        momentum_new,
    )


def solution(mesh):
    in_specs = (
        P(("replica", "fsdp"), None),
        P(("replica", "fsdp"), None),
        P("replica", "fsdp", None),
        P("replica", "fsdp", None),
        P("replica", "fsdp", None),
        P("replica", None, "fsdp"),
        P("replica", None, "fsdp"),
        P("replica", "fsdp"),
        P("replica", "fsdp"),
    )
    out_specs = (
        P(("replica", "fsdp"), None),
        P("replica", "fsdp", None),
        P("replica", "fsdp", None),
        P("replica", "fsdp", None),
        P("replica", None, "fsdp"),
        P("replica", None, "fsdp"),
        P("replica", "fsdp"),
        P("replica", "fsdp"),
    )
    return jax.shard_map(
        per_device, mesh=mesh, in_specs=in_specs, out_specs=out_specs, check_vma=False
    )
```

```python
import jax
import jax.numpy as jnp
from jax import lax
from jax.sharding import PartitionSpec as P

HEAD_SIZE = 128
QUERY_HEADS = 16
KEYVALUE_HEADS = 4


theta_base = 500000.0
momentum_decay = 0.9
outer_rate = 0.7
mixing = 0.5


def apply_rotation(value_rows, sign):
    sequence_length = value_rows.shape[0]
    half = value_rows.shape[2] // 2
    position = jnp.arange(sequence_length).astype(jnp.float32)
    freq = jnp.exp(
        -jnp.log(theta_base) * jnp.arange(half).astype(jnp.float32) * 2.0 / value_rows.shape[2]
    )
    angle = position[:, None] * freq[None, :]
    cosine = jnp.cos(angle)[:, None, :]
    sine = sign * jnp.sin(angle)[:, None, :]
    first = value_rows[..., :half]
    second = value_rows[..., half:]
    return jnp.concatenate(
        [first * cosine - second * sine, first * sine + second * cosine], axis=-1
    )


def rotate(value_rows, sign):
    return jax.vmap(lambda rows: apply_rotation(rows, sign))(value_rows)


def relay(block, tied=()):
    n = lax.axis_size("fsdp")
    me = lax.axis_index("fsdp")
    up, down = [block], [block]
    for hop in range(1, n):
        if hop == n - 1:
            last_up, last_down, tied = lax.optimization_barrier((up[-1], down[-1], tied))
        else:
            last_up, last_down = up[-1], down[-1]
        up.append(lax.ppermute(last_up, "fsdp", [(f, f + 1) for f in range(hop - 1, n - 1)]))
        down.append(lax.ppermute(last_down, "fsdp", [(f, f - 1) for f in range(1, n - hop + 1)]))
    return [block] + [jnp.where(me >= j, up[j], down[n - j]) for j in range(1, n)], tied


def gather(block, place, out, tied=()):
    n = lax.axis_size("fsdp")
    me = lax.axis_index("fsdp")
    blocks, tied = relay(block, tied)
    for j in range(n):
        out = place(out, blocks[j], lax.rem(me + n - j, n))
    return out, tied


def place_rows(out, piece, f):
    return lax.dynamic_update_slice_in_dim(out, piece, f * piece.shape[0], 0)


def place_cols(out, piece, f):
    return lax.dynamic_update_slice_in_dim(out, piece, f * piece.shape[1], 1)


def attend(query_raw, key_raw, value_raw):
    scale = HEAD_SIZE ** (-0.5)
    query_rows = rotate(query_raw, 1.0).astype(jnp.bfloat16)
    key_rows = rotate(key_raw[:, :, None, :], 1.0)[:, :, 0].astype(jnp.bfloat16)
    value_rows = value_raw.astype(jnp.bfloat16)
    length = query_raw.shape[1]
    scores = (
        jnp.einsum("sqgd,skd->sgqk", query_rows, key_rows, preferred_element_type=jnp.float32)
        * scale
    )
    causal = jnp.arange(length)[:, None] >= jnp.arange(length)[None, :]
    scores = jnp.where(causal, scores, -1e30)
    top = jnp.max(scores, axis=-1, keepdims=True)
    expo = jnp.exp(scores - top)
    probs = expo / jnp.sum(expo, axis=-1, keepdims=True)
    probs_b = probs.astype(jnp.bfloat16)
    attn = jnp.einsum("sgqk,skd->sqgd", probs_b, value_rows, preferred_element_type=jnp.float32)
    return attn.astype(jnp.bfloat16), (query_rows, key_rows, value_rows, probs, probs_b)


def attend_gradient(saved, d_attn):
    query_rows, key_rows, value_rows, probs, probs_b = saved
    scale = HEAD_SIZE ** (-0.5)
    d_values = jnp.einsum("sgqk,sqgd->skd", probs_b, d_attn, preferred_element_type=jnp.float32)
    d_probs = jnp.einsum("sqgd,skd->sgqk", d_attn, value_rows, preferred_element_type=jnp.float32)
    d_scores = (probs * (d_probs - jnp.sum(d_probs * probs, axis=-1, keepdims=True))).astype(
        jnp.bfloat16
    )
    d_queries = (
        jnp.einsum("sgqk,skd->sqgd", d_scores, key_rows, preferred_element_type=jnp.float32) * scale
    )
    d_keys = (
        jnp.einsum("sgqk,sqgd->skd", d_scores, query_rows, preferred_element_type=jnp.float32)
        * scale
    )
    d_queries = rotate(d_queries, -1.0)
    d_keys = rotate(d_keys[:, :, None, :], -1.0)[:, :, 0]
    rows = d_attn.shape[0] * d_attn.shape[1]
    return jnp.concatenate(
        [part.astype(jnp.bfloat16).reshape(rows, -1) for part in (d_queries, d_keys, d_values)],
        axis=1,
    )


def exchange(pick, place, out):
    n = lax.axis_size("fsdp")
    me = lax.axis_index("fsdp")
    out = place(out, pick(me), me)
    for shift in range(1, n):
        pairs = [(f, (f + shift) % n) for f in range(n)]
        piece = lax.ppermute(pick(lax.rem(me + shift, n)), "fsdp", pairs)
        out = place(out, piece, lax.rem(me + n - shift, n))
    return out


def outer_sync(snapshot, global_output, momentum, w_output):
    total = lax.psum_scatter(
        snapshot[0].astype(jnp.float32), "replica", scatter_dimension=0, tiled=True
    )
    mean_snapshot = total / lax.axis_size("replica")
    delta = global_output - mean_snapshot
    momentum_new = momentum_decay * momentum + delta
    global_new = global_output - outer_rate * (delta + momentum_decay * momentum_new)
    gathered = lax.all_gather(global_new, "replica", axis=0, tiled=True)
    merged = (mixing * w_output[0].astype(jnp.float32) + (1.0 - mixing) * gathered).astype(
        jnp.bfloat16
    )
    return (merged[None], global_new, momentum_new)


def per_device(
    tokens,
    cotangent,
    w_query,
    replica_key_weight,
    replica_value_weight,
    w_output,
    snapshot,
    global_output,
    momentum,
):
    n = lax.axis_size("fsdp")
    me = lax.axis_index("fsdp")
    length, width = tokens.shape
    depth = w_query.shape[1]
    own_query = w_query.shape[2] // n
    own_key = replica_key_weight.shape[2] // n
    own_cols = own_query + 2 * own_key
    group = own_query // HEAD_SIZE
    model_cols = w_output.shape[2]
    total_rows = n * length

    all_tokens, (later_cotangent, later_output) = gather(
        tokens,
        place_rows,
        jnp.zeros((total_rows, width), jnp.bfloat16),
        (cotangent, w_output),
    )
    all_cotangent, _ = gather(
        later_cotangent, place_rows, jnp.zeros((total_rows, width), jnp.bfloat16)
    )

    def pick_weight(d):
        return jnp.concatenate(
            [
                lax.dynamic_slice_in_dim(w_query[0], d * own_query, own_query, 1),
                lax.dynamic_slice_in_dim(replica_key_weight[0], d * own_key, own_key, 1),
                lax.dynamic_slice_in_dim(replica_value_weight[0], d * own_key, own_key, 1),
            ],
            axis=1,
        )

    w_in = exchange(pick_weight, place_rows, jnp.zeros((n * depth, own_cols), jnp.bfloat16))
    w_out_rows = exchange(
        lambda d: lax.dynamic_slice_in_dim(later_output[0], d * own_query, own_query, 0),
        place_cols,
        jnp.zeros((own_query, n * model_cols), jnp.bfloat16),
    )

    raw = jnp.dot(all_tokens, w_in, preferred_element_type=jnp.float32)
    query_raw = raw[:, :own_query].reshape(n, length, group, HEAD_SIZE)
    key_raw = raw[:, own_query : own_query + own_key].reshape(n, length, HEAD_SIZE)
    value_raw = raw[:, own_query + own_key :].reshape(n, length, HEAD_SIZE)
    attn, saved = attend(query_raw, key_raw, value_raw)

    own_attn = attn.reshape(total_rows, own_query)
    all_attn, _ = gather(
        own_attn, place_cols, jnp.zeros((total_rows, n * own_query), jnp.bfloat16)
    )

    d_attn = (
        lax.dot_general(
            all_cotangent,
            w_out_rows,
            (((1,), (1,)), ((), ())),
            preferred_element_type=jnp.float32,
        )
        .astype(jnp.bfloat16)
        .reshape(n, length, group, HEAD_SIZE)
    )
    d_in = attend_gradient(saved, d_attn)
    grad_in = lax.dot_general(
        all_tokens, d_in, (((0,), (0,)), ((), ())), preferred_element_type=jnp.float32
    ).astype(jnp.bfloat16)

    def place_grads(outs, piece, f):
        grad_query, grad_key, grad_value = outs
        return (
            place_cols(grad_query, piece[:, :own_query], f),
            place_cols(grad_key, piece[:, own_query : own_query + own_key], f),
            place_cols(grad_value, piece[:, own_query + own_key :], f),
        )

    grad_query, grad_key, grad_value = exchange(
        lambda d: lax.dynamic_slice_in_dim(grad_in, d * depth, depth, 0),
        place_grads,
        tuple(
            jnp.zeros(w.shape[1:], jnp.bfloat16)
            for w in (w_query, replica_key_weight, replica_value_weight)
        ),
    )

    own_token_cols = lax.dynamic_slice_in_dim(all_tokens, me * model_cols, model_cols, 1)
    out_cols = (
        own_token_cols.astype(jnp.float32)
        + jnp.dot(all_attn, w_output[0], preferred_element_type=jnp.float32)
    ).astype(jnp.bfloat16)
    block_out = exchange(
        lambda d: lax.dynamic_slice_in_dim(out_cols, d * length, length, 0),
        place_cols,
        jnp.zeros((length, width), jnp.bfloat16),
    )
    own_cotangent_cols = lax.dynamic_slice_in_dim(all_cotangent, me * model_cols, model_cols, 1)
    grad_output = lax.dot_general(
        all_attn, own_cotangent_cols, (((0,), (0,)), ((), ())), preferred_element_type=jnp.float32
    ).astype(jnp.bfloat16)

    merged_output, global_new, momentum_new = outer_sync(
        snapshot, global_output, momentum, w_output
    )
    return (
        block_out,
        grad_query[None],
        grad_key[None],
        grad_value[None],
        grad_output[None],
        merged_output,
        global_new,
        momentum_new,
    )


def solution(mesh):
    in_specs = (
        P(("replica", "fsdp"), None),
        P(("replica", "fsdp"), None),
        P("replica", "fsdp", None),
        P("replica", "fsdp", None),
        P("replica", "fsdp", None),
        P("replica", None, "fsdp"),
        P("replica", None, "fsdp"),
        P("replica", "fsdp"),
        P("replica", "fsdp"),
    )
    out_specs = (
        P(("replica", "fsdp"), None),
        P("replica", "fsdp", None),
        P("replica", "fsdp", None),
        P("replica", "fsdp", None),
        P("replica", None, "fsdp"),
        P("replica", None, "fsdp"),
        P("replica", "fsdp"),
        P("replica", "fsdp"),
    )
    return jax.shard_map(
        per_device, mesh=mesh, in_specs=in_specs, out_specs=out_specs, check_vma=False
    )
```

```python
import jax
import jax.numpy as jnp
from jax import lax
from jax.sharding import PartitionSpec as P

HEAD_SIZE = 128
QUERY_HEADS = 16
KEYVALUE_HEADS = 4


theta_base = 500000.0
momentum_decay = 0.9
outer_rate = 0.7
mixing = 0.5


def apply_rotation(value_rows, sign):
    sequence_length = value_rows.shape[0]
    half = value_rows.shape[2] // 2
    position = jnp.arange(sequence_length).astype(jnp.float32)
    freq = jnp.exp(
        -jnp.log(theta_base) * jnp.arange(half).astype(jnp.float32) * 2.0 / value_rows.shape[2]
    )
    angle = position[:, None] * freq[None, :]
    cosine = jnp.cos(angle)[:, None, :]
    sine = sign * jnp.sin(angle)[:, None, :]
    first = value_rows[..., :half]
    second = value_rows[..., half:]
    return jnp.concatenate(
        [first * cosine - second * sine, first * sine + second * cosine], axis=-1
    )


def rotate(value_rows, sign):
    return jax.vmap(lambda rows: apply_rotation(rows, sign))(value_rows)


def relay(block, tied=()):
    n = lax.axis_size("fsdp")
    me = lax.axis_index("fsdp")
    up, down = [block], [block]
    for hop in range(1, n):
        if hop == n - 1:
            last_up, last_down, tied = lax.optimization_barrier((up[-1], down[-1], tied))
        else:
            last_up, last_down = up[-1], down[-1]
        up.append(lax.ppermute(last_up, "fsdp", [(f, f + 1) for f in range(hop - 1, n - 1)]))
        down.append(lax.ppermute(last_down, "fsdp", [(f, f - 1) for f in range(1, n - hop + 1)]))
    return [block] + [jnp.where(me >= j, up[j], down[n - j]) for j in range(1, n)], tied


def gather(block, place, out, tied=()):
    n = lax.axis_size("fsdp")
    me = lax.axis_index("fsdp")
    blocks, tied = relay(block, tied)
    for j in range(n):
        out = place(out, blocks[j], lax.rem(me + n - j, n))
    return out, tied


def place_rows(out, piece, f):
    return lax.dynamic_update_slice_in_dim(out, piece, f * piece.shape[0], 0)


def place_cols(out, piece, f):
    return lax.dynamic_update_slice_in_dim(out, piece, f * piece.shape[1], 1)


def attend(query_raw, key_raw, value_raw):
    scale = HEAD_SIZE ** (-0.5)
    query_rows = rotate(query_raw, 1.0).astype(jnp.bfloat16)
    key_rows = rotate(key_raw[:, :, None, :], 1.0)[:, :, 0].astype(jnp.bfloat16)
    value_rows = value_raw.astype(jnp.bfloat16)
    length = query_raw.shape[1]
    scores = (
        jnp.einsum("sqgd,skd->sgqk", query_rows, key_rows, preferred_element_type=jnp.float32)
        * scale
    )
    causal = jnp.arange(length)[:, None] >= jnp.arange(length)[None, :]
    scores = jnp.where(causal, scores, -1e30)
    top = jnp.max(scores, axis=-1, keepdims=True)
    expo = jnp.exp(scores - top)
    probs = expo / jnp.sum(expo, axis=-1, keepdims=True)
    probs_b = probs.astype(jnp.bfloat16)
    attn = jnp.einsum("sgqk,skd->sqgd", probs_b, value_rows, preferred_element_type=jnp.float32)
    return attn.astype(jnp.bfloat16), (query_rows, key_rows, value_rows, probs, probs_b)


def score_gradient(saved, d_attn):
    _, _, value_rows, probs, _ = saved
    d_probs = jnp.einsum("sqgd,skd->sgqk", d_attn, value_rows, preferred_element_type=jnp.float32)
    return (probs * (d_probs - jnp.sum(d_probs * probs, axis=-1, keepdims=True))).astype(
        jnp.bfloat16
    )


def attend_gradient(saved, d_attn, d_scores):
    query_rows, key_rows, _, _, probs_b = saved
    scale = HEAD_SIZE ** (-0.5)
    d_values = jnp.einsum("sgqk,sqgd->skd", probs_b, d_attn, preferred_element_type=jnp.float32)
    d_queries = (
        jnp.einsum("sgqk,skd->sqgd", d_scores, key_rows, preferred_element_type=jnp.float32) * scale
    )
    d_keys = (
        jnp.einsum("sgqk,sqgd->skd", d_scores, query_rows, preferred_element_type=jnp.float32)
        * scale
    )
    d_queries = rotate(d_queries, -1.0)
    d_keys = rotate(d_keys[:, :, None, :], -1.0)[:, :, 0]
    rows = d_attn.shape[0] * d_attn.shape[1]
    return jnp.concatenate(
        [part.astype(jnp.bfloat16).reshape(rows, -1) for part in (d_queries, d_keys, d_values)],
        axis=1,
    )


def send(pick):
    n = lax.axis_size("fsdp")
    me = lax.axis_index("fsdp")
    return [
        lax.ppermute(
            pick(lax.rem(me + shift, n)), "fsdp", [(f, (f + shift) % n) for f in range(n)]
        )
        for shift in range(1, n)
    ]


def place_pieces(pick, pieces, place, out):
    n = lax.axis_size("fsdp")
    me = lax.axis_index("fsdp")
    out = place(out, pick(me), me)
    for shift, piece in enumerate(pieces, 1):
        out = place(out, piece, lax.rem(me + n - shift, n))
    return out


def exchange(pick, place, out):
    return place_pieces(pick, send(pick), place, out)


def outer_sync(snapshot, global_output, momentum, w_output):
    total = lax.psum_scatter(
        snapshot[0].astype(jnp.float32), "replica", scatter_dimension=0, tiled=True
    )
    mean_snapshot = total / lax.axis_size("replica")
    delta = global_output - mean_snapshot
    momentum_new = momentum_decay * momentum + delta
    global_new = global_output - outer_rate * (delta + momentum_decay * momentum_new)
    gathered = lax.all_gather(global_new, "replica", axis=0, tiled=True)
    merged = (mixing * w_output[0].astype(jnp.float32) + (1.0 - mixing) * gathered).astype(
        jnp.bfloat16
    )
    return (merged[None], global_new, momentum_new)


def per_device(
    tokens,
    cotangent,
    w_query,
    replica_key_weight,
    replica_value_weight,
    w_output,
    snapshot,
    global_output,
    momentum,
):
    n = lax.axis_size("fsdp")
    me = lax.axis_index("fsdp")
    length, width = tokens.shape
    depth = w_query.shape[1]
    own_query = w_query.shape[2] // n
    own_key = replica_key_weight.shape[2] // n
    own_cols = own_query + 2 * own_key
    group = own_query // HEAD_SIZE
    model_cols = w_output.shape[2]
    total_rows = n * length

    all_tokens, (later_cotangent, later_output) = gather(
        tokens,
        place_rows,
        jnp.zeros((total_rows, width), jnp.bfloat16),
        (cotangent, w_output),
    )
    all_cotangent, _ = gather(
        later_cotangent, place_rows, jnp.zeros((total_rows, width), jnp.bfloat16)
    )

    def pick_weight(d):
        return jnp.concatenate(
            [
                lax.dynamic_slice_in_dim(w_query[0], d * own_query, own_query, 1),
                lax.dynamic_slice_in_dim(replica_key_weight[0], d * own_key, own_key, 1),
                lax.dynamic_slice_in_dim(replica_value_weight[0], d * own_key, own_key, 1),
            ],
            axis=1,
        )

    w_in = exchange(pick_weight, place_rows, jnp.zeros((n * depth, own_cols), jnp.bfloat16))
    w_out_rows = exchange(
        lambda d: lax.dynamic_slice_in_dim(later_output[0], d * own_query, own_query, 0),
        place_cols,
        jnp.zeros((own_query, n * model_cols), jnp.bfloat16),
    )

    raw = jnp.dot(all_tokens, w_in, preferred_element_type=jnp.float32)
    query_raw = raw[:, :own_query].reshape(n, length, group, HEAD_SIZE)
    key_raw = raw[:, own_query : own_query + own_key].reshape(n, length, HEAD_SIZE)
    value_raw = raw[:, own_query + own_key :].reshape(n, length, HEAD_SIZE)
    attn, saved = attend(query_raw, key_raw, value_raw)

    own_attn = attn.reshape(total_rows, own_query)
    d_attn = (
        lax.dot_general(
            all_cotangent,
            w_out_rows,
            (((1,), (1,)), ((), ())),
            preferred_element_type=jnp.float32,
        )
        .astype(jnp.bfloat16)
        .reshape(n, length, group, HEAD_SIZE)
    )
    all_attn, d_scores = gather(
        own_attn,
        place_cols,
        jnp.zeros((total_rows, n * own_query), jnp.bfloat16),
        score_gradient(saved, d_attn),
    )
    d_in = attend_gradient(saved, d_attn, d_scores)
    grad_in = lax.dot_general(
        all_tokens, d_in, (((0,), (0,)), ((), ())), preferred_element_type=jnp.float32
    ).astype(jnp.bfloat16)

    def place_grads(outs, piece, f):
        grad_query, grad_key, grad_value = outs
        return (
            place_cols(grad_query, piece[:, :own_query], f),
            place_cols(grad_key, piece[:, own_query : own_query + own_key], f),
            place_cols(grad_value, piece[:, own_query + own_key :], f),
        )

    def pick_grads(d):
        return lax.dynamic_slice_in_dim(grad_in, d * depth, depth, 0)

    grad_pieces = send(pick_grads)
    own_token_cols = lax.dynamic_slice_in_dim(all_tokens, me * model_cols, model_cols, 1)
    out_cols = (
        own_token_cols.astype(jnp.float32)
        + jnp.dot(all_attn, w_output[0], preferred_element_type=jnp.float32)
    ).astype(jnp.bfloat16)
    def pick_out(d):
        return lax.dynamic_slice_in_dim(out_cols, d * length, length, 0)

    out_pieces = send(pick_out)
    grad_pieces, _ = lax.optimization_barrier((grad_pieces, out_cols))
    grad_query, grad_key, grad_value = place_pieces(
        pick_grads,
        grad_pieces,
        place_grads,
        tuple(
            jnp.zeros(w.shape[1:], jnp.bfloat16)
            for w in (w_query, replica_key_weight, replica_value_weight)
        ),
    )
    own_cotangent_cols = lax.dynamic_slice_in_dim(all_cotangent, me * model_cols, model_cols, 1)
    grad_output = lax.dot_general(
        all_attn, own_cotangent_cols, (((0,), (0,)), ((), ())), preferred_element_type=jnp.float32
    ).astype(jnp.bfloat16)

    merged_output, global_new, momentum_new = outer_sync(
        snapshot, global_output, momentum, w_output
    )
    out_pieces[0], merged_output = lax.optimization_barrier((out_pieces[0], merged_output))
    block_out = place_pieces(
        pick_out, out_pieces, place_cols, jnp.zeros((length, width), jnp.bfloat16)
    )
    return (
        block_out,
        grad_query[None],
        grad_key[None],
        grad_value[None],
        grad_output[None],
        merged_output,
        global_new,
        momentum_new,
    )


def solution(mesh):
    in_specs = (
        P(("replica", "fsdp"), None),
        P(("replica", "fsdp"), None),
        P("replica", "fsdp", None),
        P("replica", "fsdp", None),
        P("replica", "fsdp", None),
        P("replica", None, "fsdp"),
        P("replica", None, "fsdp"),
        P("replica", "fsdp"),
        P("replica", "fsdp"),
    )
    out_specs = (
        P(("replica", "fsdp"), None),
        P("replica", "fsdp", None),
        P("replica", "fsdp", None),
        P("replica", "fsdp", None),
        P("replica", None, "fsdp"),
        P("replica", None, "fsdp"),
        P("replica", "fsdp"),
        P("replica", "fsdp"),
    )
    return jax.shard_map(
        per_device, mesh=mesh, in_specs=in_specs, out_specs=out_specs, check_vma=False
    )
```

```python
import jax
import jax.numpy as jnp
from jax import lax
from jax.sharding import PartitionSpec as P

HEAD_SIZE = 128
QUERY_HEADS = 16
KEYVALUE_HEADS = 4


theta_base = 500000.0
momentum_decay = 0.9
outer_rate = 0.7
mixing = 0.5


def apply_rotation(value_rows, sign):
    sequence_length = value_rows.shape[0]
    half = value_rows.shape[2] // 2
    position = jnp.arange(sequence_length).astype(jnp.float32)
    freq = jnp.exp(
        -jnp.log(theta_base) * jnp.arange(half).astype(jnp.float32) * 2.0 / value_rows.shape[2]
    )
    angle = position[:, None] * freq[None, :]
    cosine = jnp.cos(angle)[:, None, :]
    sine = sign * jnp.sin(angle)[:, None, :]
    first = value_rows[..., :half]
    second = value_rows[..., half:]
    return jnp.concatenate(
        [first * cosine - second * sine, first * sine + second * cosine], axis=-1
    )


def rotate(value_rows, sign):
    return jax.vmap(lambda rows: apply_rotation(rows, sign))(value_rows)


def relay(block, tied=()):
    n = lax.axis_size("fsdp")
    me = lax.axis_index("fsdp")
    up, down = [block], [block]
    for hop in range(1, n):
        if hop == n - 1:
            last_up, last_down, tied = lax.optimization_barrier((up[-1], down[-1], tied))
        else:
            last_up, last_down = up[-1], down[-1]
        up.append(lax.ppermute(last_up, "fsdp", [(f, f + 1) for f in range(hop - 1, n - 1)]))
        down.append(lax.ppermute(last_down, "fsdp", [(f, f - 1) for f in range(1, n - hop + 1)]))
    return [block] + [jnp.where(me >= j, up[j], down[n - j]) for j in range(1, n)], tied


def gather(block, place, out, tied=()):
    n = lax.axis_size("fsdp")
    me = lax.axis_index("fsdp")
    blocks, tied = relay(block, tied)
    for j in range(n):
        out = place(out, blocks[j], lax.rem(me + n - j, n))
    return out, tied


def place_rows(out, piece, f):
    return lax.dynamic_update_slice_in_dim(out, piece, f * piece.shape[0], 0)


def place_cols(out, piece, f):
    return lax.dynamic_update_slice_in_dim(out, piece, f * piece.shape[1], 1)


def attend(query_raw, key_raw, value_raw):
    scale = HEAD_SIZE ** (-0.5)
    query_rows = rotate(query_raw, 1.0).astype(jnp.bfloat16)
    key_rows = rotate(key_raw[:, :, None, :], 1.0)[:, :, 0].astype(jnp.bfloat16)
    value_rows = value_raw.astype(jnp.bfloat16)
    length = query_raw.shape[1]
    scores = (
        jnp.einsum("sqgd,skd->sgqk", query_rows, key_rows, preferred_element_type=jnp.float32)
        * scale
    )
    causal = jnp.arange(length)[:, None] >= jnp.arange(length)[None, :]
    scores = jnp.where(causal, scores, -1e30)
    top = jnp.max(scores, axis=-1, keepdims=True)
    expo = jnp.exp(scores - top)
    probs = expo / jnp.sum(expo, axis=-1, keepdims=True)
    probs_b = probs.astype(jnp.bfloat16)
    attn = jnp.einsum("sgqk,skd->sqgd", probs_b, value_rows, preferred_element_type=jnp.float32)
    return attn.astype(jnp.bfloat16), (query_rows, key_rows, value_rows, probs, probs_b)


def score_gradient(saved, d_attn):
    _, _, value_rows, probs, _ = saved
    d_probs = jnp.einsum("sqgd,skd->sgqk", d_attn, value_rows, preferred_element_type=jnp.float32)
    return (probs * (d_probs - jnp.sum(d_probs * probs, axis=-1, keepdims=True))).astype(
        jnp.bfloat16
    )


def attend_gradient(saved, d_attn, d_scores):
    query_rows, key_rows, _, _, probs_b = saved
    scale = HEAD_SIZE ** (-0.5)
    d_values = jnp.einsum("sgqk,sqgd->skd", probs_b, d_attn, preferred_element_type=jnp.float32)
    d_queries = (
        jnp.einsum("sgqk,skd->sqgd", d_scores, key_rows, preferred_element_type=jnp.float32) * scale
    )
    d_keys = (
        jnp.einsum("sgqk,sqgd->skd", d_scores, query_rows, preferred_element_type=jnp.float32)
        * scale
    )
    d_queries = rotate(d_queries, -1.0)
    d_keys = rotate(d_keys[:, :, None, :], -1.0)[:, :, 0]
    rows = d_attn.shape[0] * d_attn.shape[1]
    return jnp.concatenate(
        [part.astype(jnp.bfloat16).reshape(rows, -1) for part in (d_queries, d_keys, d_values)],
        axis=1,
    )


def send(pick):
    n = lax.axis_size("fsdp")
    me = lax.axis_index("fsdp")
    return [
        lax.ppermute(
            pick(lax.rem(me + shift, n)), "fsdp", [(f, (f + shift) % n) for f in range(n)]
        )
        for shift in range(1, n)
    ]


def place_pieces(pick, pieces, place, out):
    n = lax.axis_size("fsdp")
    me = lax.axis_index("fsdp")
    out = place(out, pick(me), me)
    for shift, piece in enumerate(pieces, 1):
        out = place(out, piece, lax.rem(me + n - shift, n))
    return out


def exchange(pick, place, out):
    return place_pieces(pick, send(pick), place, out)


def outer_sync(snapshot, global_output, momentum, w_output):
    total = lax.psum_scatter(
        snapshot[0].astype(jnp.float32), "replica", scatter_dimension=0, tiled=True
    )
    mean_snapshot = total / lax.axis_size("replica")
    delta = global_output - mean_snapshot
    momentum_new = momentum_decay * momentum + delta
    global_new = global_output - outer_rate * (delta + momentum_decay * momentum_new)
    gathered = lax.all_gather(global_new, "replica", axis=0, tiled=True)
    merged = (mixing * w_output[0].astype(jnp.float32) + (1.0 - mixing) * gathered).astype(
        jnp.bfloat16
    )
    return (merged[None], global_new, momentum_new)


def per_device(
    tokens,
    cotangent,
    w_query,
    replica_key_weight,
    replica_value_weight,
    w_output,
    snapshot,
    global_output,
    momentum,
):
    n = lax.axis_size("fsdp")
    me = lax.axis_index("fsdp")
    length, width = tokens.shape
    depth = w_query.shape[1]
    own_query = w_query.shape[2] // n
    own_key = replica_key_weight.shape[2] // n
    own_cols = own_query + 2 * own_key
    group = own_query // HEAD_SIZE
    model_cols = w_output.shape[2]
    total_rows = n * length

    all_tokens, (later_cotangent, later_output) = gather(
        tokens,
        place_rows,
        jnp.zeros((total_rows, width), jnp.bfloat16),
        (cotangent, w_output),
    )
    cotangent_blocks, _ = relay(later_cotangent)
    all_cotangent = jnp.zeros((total_rows, width), jnp.bfloat16)
    for j in range(n):
        all_cotangent = place_rows(all_cotangent, cotangent_blocks[j], lax.rem(me + n - j, n))

    def pick_weight(d):
        return jnp.concatenate(
            [
                lax.dynamic_slice_in_dim(w_query[0], d * own_query, own_query, 1),
                lax.dynamic_slice_in_dim(replica_key_weight[0], d * own_key, own_key, 1),
                lax.dynamic_slice_in_dim(replica_value_weight[0], d * own_key, own_key, 1),
            ],
            axis=1,
        )

    w_in = exchange(pick_weight, place_rows, jnp.zeros((n * depth, own_cols), jnp.bfloat16))
    w_out_rows = exchange(
        lambda d: lax.dynamic_slice_in_dim(later_output[0], d * own_query, own_query, 0),
        place_cols,
        jnp.zeros((own_query, n * model_cols), jnp.bfloat16),
    )

    raw = jnp.dot(all_tokens, w_in, preferred_element_type=jnp.float32)
    query_raw = raw[:, :own_query].reshape(n, length, group, HEAD_SIZE)
    key_raw = raw[:, own_query : own_query + own_key].reshape(n, length, HEAD_SIZE)
    value_raw = raw[:, own_query + own_key :].reshape(n, length, HEAD_SIZE)
    attn, saved = attend(query_raw, key_raw, value_raw)

    own_attn = attn.reshape(total_rows, own_query)
    d_attn = jnp.zeros((total_rows, own_query), jnp.bfloat16)
    for j in (0, 1, 3, 2) if n == 4 else range(n):
        part = lax.dot_general(
            cotangent_blocks[j],
            w_out_rows,
            (((1,), (1,)), ((), ())),
            preferred_element_type=jnp.float32,
        ).astype(jnp.bfloat16)
        d_attn = place_rows(d_attn, part, lax.rem(me + n - j, n))
    d_attn = d_attn.reshape(n, length, group, HEAD_SIZE)
    all_attn, d_scores = gather(
        own_attn,
        place_cols,
        jnp.zeros((total_rows, n * own_query), jnp.bfloat16),
        score_gradient(saved, d_attn),
    )
    d_in = attend_gradient(saved, d_attn, d_scores)
    grad_in = lax.dot_general(
        all_tokens, d_in, (((0,), (0,)), ((), ())), preferred_element_type=jnp.float32
    ).astype(jnp.bfloat16)

    def place_grads(outs, piece, f):
        grad_query, grad_key, grad_value = outs
        return (
            place_cols(grad_query, piece[:, :own_query], f),
            place_cols(grad_key, piece[:, own_query : own_query + own_key], f),
            place_cols(grad_value, piece[:, own_query + own_key :], f),
        )

    def pick_grads(d):
        return lax.dynamic_slice_in_dim(grad_in, d * depth, depth, 0)

    grad_pieces = send(pick_grads)
    own_token_cols = lax.dynamic_slice_in_dim(all_tokens, me * model_cols, model_cols, 1)
    out_cols = (
        own_token_cols.astype(jnp.float32)
        + jnp.dot(all_attn, w_output[0], preferred_element_type=jnp.float32)
    ).astype(jnp.bfloat16)
    def pick_out(d):
        return lax.dynamic_slice_in_dim(out_cols, d * length, length, 0)

    out_pieces = send(pick_out)
    grad_pieces, _ = lax.optimization_barrier((grad_pieces, out_cols))
    grad_query, grad_key, grad_value = place_pieces(
        pick_grads,
        grad_pieces,
        place_grads,
        tuple(
            jnp.zeros(w.shape[1:], jnp.bfloat16)
            for w in (w_query, replica_key_weight, replica_value_weight)
        ),
    )
    own_cotangent_cols = lax.dynamic_slice_in_dim(all_cotangent, me * model_cols, model_cols, 1)
    grad_output = lax.dot_general(
        all_attn, own_cotangent_cols, (((0,), (0,)), ((), ())), preferred_element_type=jnp.float32
    ).astype(jnp.bfloat16)

    merged_output, global_new, momentum_new = outer_sync(
        snapshot, global_output, momentum, w_output
    )
    out_pieces[0], merged_output = lax.optimization_barrier((out_pieces[0], merged_output))
    block_out = place_pieces(
        pick_out, out_pieces, place_cols, jnp.zeros((length, width), jnp.bfloat16)
    )
    return (
        block_out,
        grad_query[None],
        grad_key[None],
        grad_value[None],
        grad_output[None],
        merged_output,
        global_new,
        momentum_new,
    )


def solution(mesh):
    in_specs = (
        P(("replica", "fsdp"), None),
        P(("replica", "fsdp"), None),
        P("replica", "fsdp", None),
        P("replica", "fsdp", None),
        P("replica", "fsdp", None),
        P("replica", None, "fsdp"),
        P("replica", None, "fsdp"),
        P("replica", "fsdp"),
        P("replica", "fsdp"),
    )
    out_specs = (
        P(("replica", "fsdp"), None),
        P("replica", "fsdp", None),
        P("replica", "fsdp", None),
        P("replica", "fsdp", None),
        P("replica", None, "fsdp"),
        P("replica", None, "fsdp"),
        P("replica", "fsdp"),
        P("replica", "fsdp"),
    )
    return jax.shard_map(
        per_device, mesh=mesh, in_specs=in_specs, out_specs=out_specs, check_vma=False
    )
```
